32 devices in a mesh: groups: 2 (over y), col: 4 (over z), row: 2 (over x), sub: 2 (over core).
Axes of the slice: x: 2, y: 2, z: 4, core: 2. Of those that a mesh axis runs over, the one named last changes fastest.
Arguments:
- amps: float32 [1536, 69632], P(('groups', 'row'), ('col', 'sub')), parts along dimension 0, may hold values from -12 to 12
- integrals: float32 [139264, 1024], P(('groups', 'col', 'sub')), parts along dimension 0, may hold values from -0.03125 to 0.03125
- occ_pairs: int32 [768, 2], P('row'), may hold values from 0 to 63, as said below
- slab_pairs: int32 [1024, 2], replicated, may hold values from 0 to 511, as said below
- occ_energy: float32 [128], P('groups'), parts along dimension 0, may hold values from -1.2 to -0.3
- vir_energy: float32 [1024], P('groups'), parts along dimension 0, may hold values from 0.1 to 1.5
Outputs:
- residual: float32 [1536, 1024], P(('groups', 'row'), ('col', 'sub')), parts along dimension 0
- increment: float32 [1536, 1024], P(('groups', 'row'), ('col', 'sub')), parts along dimension 0
The draws below stay inside these ranges and needn't reach their ends.
There are 2 independent parts, one for each index of `groups`. The reference program is written for one: setup_inputs(seed, part) draws one part's arguments, and reference() takes and returns one part's arrays. A program takes and returns all parts, laid end to end along the dimension named above; an argument that names none is the same for every part. Nothing has to cross between parts.
Inputs may be any that keep to these rules, and one draw needn't show every extreme that they name: `occ_pairs`: each row holds two occupied orbitals, the first no larger than the second. `slab_pairs`: each row holds two virtual orbitals, the first no larger than the second.
All inputs are finite; a program needn't handle non-finite values.
Results may differ from the reference program's by a relative error of at most 0.000073.
Values sent between devices are 32-bit elements; how exact they have to be, the bound alone decides.
A program may use at most 128 MiB of HBM per device.

```python
import jax
import jax.numpy as jnp
from jax import lax

NOCC = 64
NVIR = 512
KPAIRS = 69632
NSLAB = 1024
PAIRS = 768


def ordered_pairs(key, count, limit):
    first_key, second_key = jax.random.split(key)
    first = jax.random.randint(first_key, (count,), 0, limit).astype(jnp.int32)
    second = jax.random.randint(second_key, (count,), 0, limit).astype(jnp.int32)
    lower = jnp.minimum(first, second).at[0].set(0)
    upper = jnp.maximum(first, second).at[0].set(limit - 1)
    return jnp.stack([lower, upper], axis=1).astype(jnp.int32)


def draw_occ_pairs(key, part):
    key = jax.random.fold_in(key, 11)
    return ordered_pairs(key, PAIRS, NOCC)


def draw_slab_pairs(key, part):
    key = jax.random.fold_in(key, 23)
    return ordered_pairs(key, NSLAB, NVIR)


def spiked(drawn, key, source, target, shards_of, factor):
    def block_of(axis_at):
        return (jnp.arange(drawn.shape[axis_at]) // (drawn.shape[axis_at] // shards_of)).reshape((-1,) + (1,) * (drawn.ndim - 1 - axis_at))

    one_side = jax.random.permutation(key, shards_of)[block_of(target)]
    other_side = (block_of(target) + shards_of // 2) % shards_of
    return jnp.where((block_of(source) == one_side) | (block_of(source) == other_side), factor * drawn, drawn)


def block_levels(stream_key, shape, shards, smallest, top_value):
    def one(position, shards_of):
        steps = jax.random.uniform(jax.random.fold_in(jax.random.fold_in(stream_key, 6), position), (shards_of,), jnp.float32, smallest / len(shards), top_value / len(shards))
        return jnp.repeat(jnp.exp(steps), shape[position] // shards_of).reshape((-1,) + (1,) * (len(shape) - position - 1))

    gain = one(*shards[0])
    for cut in shards[1:]:
        gain = gain * one(*cut)
    return gain


def centred(rng, extent, width, bound, cuts=(), dtype=jnp.bfloat16):
    values = width * jax.random.normal(rng, extent, jnp.float32)
    if cuts:
        values = values * block_levels(rng, extent, cuts, -0.22, 0.18)
    return jnp.clip(values, -bound, bound).astype(dtype)


def noise_with(stream_key, dims, spread, reach, shards, heavy, held_as=jnp.bfloat16):
    result = spread * jax.random.normal(stream_key, dims, jnp.float32)
    if shards:
        result = result * block_levels(stream_key, dims, shards, -0.22, 0.18)
    return jnp.clip(spiked(result, jax.random.fold_in(stream_key, 3), *heavy), -reach, reach).astype(held_as)


def setup_inputs(seed: int = 0, part: int = 0) -> dict:
    keys = jax.random.split(jax.random.key(seed), 7)
    own_keys = jax.random.split(jax.random.fold_in(keys[6], part), 7)
    amps = centred(own_keys[0], (PAIRS, KPAIRS), 2.0, 12.0, ((0, 2), (1, 8)), jnp.float32)
    integrals = noise_with(own_keys[1], (KPAIRS, NSLAB), KPAIRS ** -0.5, 0.03125, ((0, 8),), (0, 1, 8, 2.0), jnp.float32)
    occ_pairs = draw_occ_pairs(jax.random.fold_in(keys[6], 71), part)
    slab_pairs = draw_slab_pairs(jax.random.fold_in(keys[6], 71), part)
    occ_energy = jnp.clip(jax.random.uniform(own_keys[4], (NOCC,), jnp.float32, -1.2, -0.3), -1.2, -0.3)
    vir_energy = jnp.clip(jax.random.uniform(own_keys[5], (NVIR,), jnp.float32, 0.1, 1.5), 0.1, 1.5)
    return dict(amps=amps, integrals=integrals, occ_pairs=occ_pairs, slab_pairs=slab_pairs, occ_energy=occ_energy, vir_energy=vir_energy)


def reference(amps, integrals, occ_pairs, slab_pairs, occ_energy, vir_energy):
    residual = jnp.dot(amps, integrals, precision=lax.Precision.HIGHEST, preferred_element_type=jnp.float32)
    occ_sum = occ_energy[occ_pairs[:, 0]] + occ_energy[occ_pairs[:, 1]]
    vir_sum = vir_energy[slab_pairs[:, 0]] + vir_energy[slab_pairs[:, 1]]
    denominator = occ_sum[:, None] - vir_sum[None, :]
    increment = residual / denominator
    return residual, increment
```

```python
import functools

import jax
import jax.numpy as jnp
from jax import lax
from jax.experimental import pallas as pl
from jax.experimental.pallas import tpu as pltpu
from jax.sharding import PartitionSpec as P

LANES = 128
CHUNKS = 17
MESH = pl.DeviceIdType.MESH


def lookup(table, indices):
    places = jnp.arange(table.shape[0], dtype=jnp.int32)
    return jnp.sum(jnp.where(indices[:, None] == places[None, :], table[None, :], 0.0), axis=1)


def pair_energy(table, pairs):
    return lookup(table, pairs[:, 0]) + lookup(table, pairs[:, 1])


def plain(amps, integrals, occ_pairs, slab_pairs, occ_energy, vir_energy):
    width = integrals.shape[1]
    pieces = lax.axis_size(("col", "sub"))
    partial_value = jnp.dot(
        amps, integrals, precision=lax.Precision.HIGH, preferred_element_type=jnp.float32
    )
    residual = lax.psum_scatter(partial_value, ("col", "sub"), scatter_dimension=1, tiled=True)
    columns = width // pieces
    first_col = lax.axis_index(("col", "sub")) * columns
    slab_here = lax.dynamic_slice_in_dim(slab_pairs, first_col, columns, 0)
    denominator = (
        pair_energy(occ_energy, occ_pairs)[:, None] - pair_energy(vir_energy, slab_here)[None, :]
    )
    increment = residual / denominator
    return (residual, increment)


def column_of(row):
    n = row.shape[1]
    here = lax.broadcasted_iota(jnp.int32, (n, n), 0) == lax.broadcasted_iota(jnp.int32, (n, n), 1)
    return jnp.sum(jnp.where(here, jnp.broadcast_to(row, (n, n)), 0.0), axis=1, keepdims=True)


def table_row(table, indices):
    shape = (table.shape[0], indices.shape[1])
    places = lax.broadcasted_iota(jnp.int32, shape, 0)
    picked = jnp.where(places == jnp.broadcast_to(indices, shape), jnp.broadcast_to(table, shape), 0.0)
    return jnp.sum(picked, axis=0, keepdims=True)


def split(values):
    high = values.astype(jnp.bfloat16)
    return high, (values - high.astype(jnp.float32)).astype(jnp.bfloat16)


def dot(a, b):
    return jnp.dot(a, b, preferred_element_type=jnp.float32)


def ladder(
    cols_n, amps, integrals, occ_t, slab_t, occ_e, vir_e, residual, increment,
    wide, halves, blocks, acc, denom, outbox, inbox, mine, arrived,
    wide_sem, block_sem, swap_send, swap_recv, hop_send, hop_recv,
):
    rows = amps.shape[0]
    depth = wide.shape[2]
    last = cols_n - 1
    col, sub = lax.axis_index("col"), lax.axis_index("sub")

    def order(j):
        return (last * (1 - col // 2), (3 * col + 2) % 5, 1 + col % 2, col)[j]

    def way(j):
        return (col // 2, col % 2, col // 2)[j]

    def load_wide(k):
        return pltpu.make_async_copy(
            amps.at[:, pl.ds(pl.multiple_of(k * depth, depth), depth)], wide.at[k], wide_sem.at[k]
        )

    def load_block(j, k):
        return pltpu.make_async_copy(
            integrals.at[
                pl.ds(pl.multiple_of(k * depth, depth), depth),
                pl.ds(pl.multiple_of(order(j) * 2 * LANES, 2 * LANES), 2 * LANES),
            ],
            blocks.at[j % 2, k],
            block_sem.at[j % 2, k],
        )

    def swap(j):
        return pltpu.make_async_remote_copy(
            src_ref=outbox.at[j], dst_ref=inbox.at[j],
            send_sem=swap_send.at[j], recv_sem=swap_recv.at[j],
            device_id={"sub": 1 - sub}, device_id_type=MESH,
        )

    def hop(j):
        return pltpu.make_async_remote_copy(
            src_ref=mine.at[j], dst_ref=arrived.at[way(j), order(j)],
            send_sem=hop_send.at[j], recv_sem=hop_recv.at[way(j), order(j)],
            device_id={"col": col + 1 - 2 * way(j)}, device_id_type=MESH,
        )

    def arrival(d, target):
        return pltpu.make_async_remote_copy(
            src_ref=mine.at[0], dst_ref=arrived.at[d, target],
            send_sem=hop_send.at[0], recv_sem=hop_recv.at[d, target],
            device_id={"col": col}, device_id_type=MESH,
        )

    @pl.loop(0, CHUNKS)
    def _(k):
        load_wide(k).start()
        load_block(0, k).start()

    @pl.loop(0, CHUNKS)
    def _(k):
        load_block(1, k).start()

    barrier = pltpu.get_barrier_semaphore()
    inner = (col > 0) & (col < last)
    pl.semaphore_signal(barrier, inc=1, device_id={"sub": 1 - sub}, device_id_type=MESH)

    @pl.when(col > 0)
    def _():
        pl.semaphore_signal(barrier, inc=1, device_id={"col": col - 1}, device_id_type=MESH)

    @pl.when(col < last)
    def _():
        pl.semaphore_signal(barrier, inc=1, device_id={"col": col + 1}, device_id_type=MESH)

    occ_table = column_of(occ_e[...])
    vir_table = jnp.concatenate(
        [column_of(vir_e[:, at : at + LANES]) for at in range(0, vir_e.shape[1], LANES)], axis=0
    )
    own = pl.multiple_of((2 * col + sub) * LANES, LANES)
    slab = slab_t[:, pl.ds(own, LANES)]
    vir_row = table_row(vir_table, slab[0:1, :]) + table_row(vir_table, slab[1:2, :])
    for at in range(0, rows, LANES):
        pairs = occ_t[:, at : at + LANES]
        occ_row = table_row(occ_table, pairs[0:1, :]) + table_row(occ_table, pairs[1:2, :])
        denom[at : at + LANES, :] = column_of(occ_row) - vir_row

    @pl.when(inner)
    def _():
        pl.semaphore_wait(barrier, 3)

    @pl.when(jnp.logical_not(inner))
    def _():
        pl.semaphore_wait(barrier, 2)

    def multiply(j, k):
        load_block(j, k).wait()
        if j == 0:
            load_wide(k).wait()
            a_high, a_low = split(wide[k])
            halves[k, :rows, :] = a_high
            halves[k, rows:, :] = a_low
        b_high, b_low = split(blocks[j % 2, k])
        both = dot(halves[k], b_high)
        term = both[:rows] + both[rows:] + dot(halves[k, :rows, :], b_low)
        acc[...] += term
        if j + 2 < cols_n:
            load_block(j + 2, k).start()

    def gather_swap(j):
        swap(j).wait_recv()
        mine[j] += inbox[j]

    def forward(j):
        arrival(way(j), order(j)).wait_recv()
        mine[j] += arrived[way(j), order(j)]
        hop(j).start()

    early, mid = 6, 10
    for j in range(cols_n):
        acc[...] = jnp.zeros_like(acc)

        @pl.loop(0, early)
        def _(k):
            multiply(j, k)

        if j >= 1:
            gather_swap(j - 1)

            @pl.when(jnp.logical_not(inner))
            def _():
                hop(j - 1).start()

        @pl.loop(early, mid)
        def _(k):
            multiply(j, k)

        if j >= 2:

            @pl.when(inner)
            def _():
                forward(j - 2)

        @pl.loop(mid, CHUNKS)
        def _(k):
            multiply(j, k)

        left, right = acc[:, :LANES], acc[:, LANES:]
        first = sub == 0
        mine[j] = jnp.where(first, left, right)
        outbox[j] = jnp.where(first, right, left)
        swap(j).start()

    @pl.when(inner)
    def _():
        forward(cols_n - 2)

    gather_swap(last)

    @pl.when(col > 0)
    def _():
        arrival(0, col).wait_recv()
        mine[last] += arrived[0, col]

    @pl.when(col < last)
    def _():
        arrival(1, col).wait_recv()
        mine[last] += arrived[1, col]

    total = mine[last]
    residual[...] = total
    increment[...] = total / denom[...]
    for j in range(cols_n):
        swap(j).wait_send()
        if j < last:
            hop(j).wait_send()


def local(amps, integrals, occ_pairs, slab_pairs, occ_energy, vir_energy):
    rows, depth = amps.shape
    width = integrals.shape[1]
    cols_n, subs = lax.axis_size("col"), lax.axis_size("sub")
    fits = (
        cols_n == 4 and subs == 2 and width == cols_n * subs * LANES
        and depth % (CHUNKS * LANES) == 0 and rows % LANES == 0
        and vir_energy.shape[0] % LANES == 0
    )
    if not fits:
        return plain(amps, integrals, occ_pairs, slab_pairs, occ_energy, vir_energy)
    piece = depth // CHUNKS
    f32, bf16 = jnp.float32, jnp.bfloat16
    dma = pltpu.SemaphoreType.DMA
    vmem = pl.BlockSpec(memory_space=pltpu.VMEM)
    hbm = pl.BlockSpec(memory_space=pl.ANY)
    return pl.pallas_call(
        functools.partial(ladder, cols_n),
        out_shape=[jax.ShapeDtypeStruct((rows, LANES), f32)] * 2,
        in_specs=[hbm, hbm, vmem, vmem, vmem, vmem],
        out_specs=[vmem, vmem],
        scratch_shapes=[
            pltpu.VMEM((CHUNKS, rows, piece), f32),
            pltpu.VMEM((CHUNKS, 2 * rows, piece), bf16),
            pltpu.VMEM((2, CHUNKS, piece, 2 * LANES), f32),
            pltpu.VMEM((rows, 2 * LANES), f32),
            pltpu.VMEM((rows, LANES), f32),
            pltpu.VMEM((cols_n, rows, LANES), f32),
            pltpu.VMEM((cols_n, rows, LANES), f32),
            pltpu.VMEM((cols_n, rows, LANES), f32),
            pltpu.VMEM((2, cols_n, rows, LANES), f32),
            dma((CHUNKS,)),
            dma((2, CHUNKS)),
            dma((cols_n,)),
            dma((cols_n,)),
            dma((cols_n,)),
            dma((2, cols_n)),
        ],
        compiler_params=pltpu.CompilerParams(
            collective_id=0, has_side_effects=True, vmem_limit_bytes=60 * 1024 * 1024
        ),
        cost_estimate=pl.CostEstimate(
            flops=6 * rows * depth * width,
            bytes_accessed=4 * depth * (rows + width),
            transcendentals=0,
        ),
    )(amps, integrals, occ_pairs.T, slab_pairs.T, occ_energy[None, :], vir_energy[None, :])


def solution(mesh):
    return jax.shard_map(
        local,
        mesh=mesh,
        in_specs=(
            P(("groups", "row"), ("col", "sub")),
            P(("groups", "col", "sub"), None),
            P("row", None),
            P(),
            P("groups"),
            P("groups"),
        ),
        out_specs=(P(("groups", "row"), ("col", "sub")), P(("groups", "row"), ("col", "sub"))),
        check_vma=False,
    )
```

```python
import functools

import jax
import jax.numpy as jnp
from jax import lax
from jax.experimental import pallas as pl
from jax.experimental.pallas import tpu as pltpu
from jax.sharding import PartitionSpec as P

LANES = 128
CHUNKS = 4
FORWARD = ((9, 0), (13, 1), (14, 2))
MESH = pl.DeviceIdType.MESH


def lookup(table, indices):
    places = jnp.arange(table.shape[0], dtype=jnp.int32)
    return jnp.sum(jnp.where(indices[:, None] == places[None, :], table[None, :], 0.0), axis=1)


def pair_energy(table, pairs):
    return lookup(table, pairs[:, 0]) + lookup(table, pairs[:, 1])


def plain(amps, integrals, occ_pairs, slab_pairs, occ_energy, vir_energy):
    width = integrals.shape[1]
    pieces = lax.axis_size(("col", "sub"))
    partial_value = jnp.dot(
        amps, integrals, precision=lax.Precision.HIGH, preferred_element_type=jnp.float32
    )
    residual = lax.psum_scatter(partial_value, ("col", "sub"), scatter_dimension=1, tiled=True)
    columns = width // pieces
    first_col = lax.axis_index(("col", "sub")) * columns
    slab_here = lax.dynamic_slice_in_dim(slab_pairs, first_col, columns, 0)
    denominator = (
        pair_energy(occ_energy, occ_pairs)[:, None] - pair_energy(vir_energy, slab_here)[None, :]
    )
    increment = residual / denominator
    return (residual, increment)


def column_of(row):
    n = row.shape[1]
    here = lax.broadcasted_iota(jnp.int32, (n, n), 0) == lax.broadcasted_iota(jnp.int32, (n, n), 1)
    return jnp.sum(jnp.where(here, jnp.broadcast_to(row, (n, n)), 0.0), axis=1, keepdims=True)


def table_row(table, indices):
    shape = (table.shape[0], indices.shape[1])
    places = lax.broadcasted_iota(jnp.int32, shape, 0)
    picked = jnp.where(places == jnp.broadcast_to(indices, shape), jnp.broadcast_to(table, shape), 0.0)
    return jnp.sum(picked, axis=0, keepdims=True)


def split(values):
    high = values.astype(jnp.bfloat16)
    return high, (values - high.astype(jnp.float32)).astype(jnp.bfloat16)


def dot(a, b):
    return jnp.dot(a, b, preferred_element_type=jnp.float32)


def ladder(
    cols_n, amps, integrals, occ_t, slab_t, occ_e, vir_e, near, far, denom,
    wide, left_hand, blocks, acc, outbox, inbox, mine, arrived,
    wide_sem, block_sem, swap_send, swap_recv, hop_send, hop_recv,
):
    rows = amps.shape[0]
    depth = wide.shape[2]
    last = cols_n - 1
    col, sub = lax.axis_index("col"), lax.axis_index("sub")

    def order(j):
        return (
            (1 - (j + 2) // 3) * last * (1 - col // 2)
            + (j % 2) * (1 - j // 3) * ((3 * col + 2) % 5)
            + (1 - j % 2) * (j // 2) * (1 + col % 2)
            + (j // 3) * col
        )

    def way(j):
        return (1 - j % 2) * (col // 2) + (j % 2) * (col % 2)

    def load_wide(k):
        return pltpu.make_async_copy(
            amps.at[:, pl.ds(pl.multiple_of(k * depth, depth), depth)], wide.at[k], wide_sem.at[k]
        )

    def load_block(step):
        j, k = step // CHUNKS, step % CHUNKS
        slot = step % (2 * CHUNKS)
        return pltpu.make_async_copy(
            integrals.at[
                pl.ds(pl.multiple_of(k * depth, depth), depth),
                pl.ds(pl.multiple_of(order(j) * 2 * LANES, 2 * LANES), 2 * LANES),
            ],
            blocks.at[slot],
            block_sem.at[slot],
        )

    def swap(j):
        return pltpu.make_async_remote_copy(
            src_ref=outbox.at[j], dst_ref=inbox.at[j],
            send_sem=swap_send.at[j], recv_sem=swap_recv.at[j],
            device_id={"sub": 1 - sub}, device_id_type=MESH,
        )

    def hop(j):
        return pltpu.make_async_remote_copy(
            src_ref=mine.at[j], dst_ref=arrived.at[way(j), order(j)],
            send_sem=hop_send.at[j], recv_sem=hop_recv.at[way(j), order(j)],
            device_id={"col": col + 1 - 2 * way(j)}, device_id_type=MESH,
        )

    def arrival(d, target):
        return pltpu.make_async_remote_copy(
            src_ref=mine.at[0], dst_ref=arrived.at[d, target],
            send_sem=hop_send.at[0], recv_sem=hop_recv.at[d, target],
            device_id={"col": col}, device_id_type=MESH,
        )

    @pl.loop(0, CHUNKS)
    def _(k):
        load_wide(k).start()
        load_block(k).start()

    @pl.loop(CHUNKS, 2 * CHUNKS)
    def _(k):
        load_block(k).start()

    barrier = pltpu.get_barrier_semaphore()
    inner = (col > 0) & (col < last)
    pl.semaphore_signal(barrier, inc=1, device_id={"sub": 1 - sub}, device_id_type=MESH)

    @pl.when(col > 0)
    def _():
        pl.semaphore_signal(barrier, inc=1, device_id={"col": col - 1}, device_id_type=MESH)

    @pl.when(col < last)
    def _():
        pl.semaphore_signal(barrier, inc=1, device_id={"col": col + 1}, device_id_type=MESH)

    occ_table = column_of(occ_e[...])
    vir_table = jnp.concatenate(
        [column_of(vir_e[:, at : at + LANES]) for at in range(0, vir_e.shape[1], LANES)], axis=0
    )
    own = pl.multiple_of((2 * col + sub) * LANES, LANES)
    slab = slab_t[:, pl.ds(own, LANES)]
    vir_row = table_row(vir_table, slab[0:1, :]) + table_row(vir_table, slab[1:2, :])
    for at in range(0, rows, LANES):
        pairs = occ_t[:, at : at + LANES]
        occ_row = table_row(occ_table, pairs[0:1, :]) + table_row(occ_table, pairs[1:2, :])
        denom[at : at + LANES, :] = column_of(occ_row) - vir_row

    @pl.when(inner)
    def _():
        pl.semaphore_wait(barrier, 3)

    @pl.when(jnp.logical_not(inner))
    def _():
        pl.semaphore_wait(barrier, 2)

    def gather_swap(j):
        swap(j).wait_recv()
        mine[j] += inbox[j]

    def forward(j):
        arrival(way(j), order(j)).wait_recv()
        mine[j] += arrived[way(j), order(j)]
        hop(j).start()

    steps = cols_n * CHUNKS

    @pl.loop(0, steps)
    def _(step):
        j, k = step // CHUNKS, step % CHUNKS
        slot = step % (2 * CHUNKS)

        @pl.when(step < CHUNKS)
        def _():
            load_wide(k).wait()
            high, low = split(wide[k])
            left_hand[k, :, :depth] = high
            left_hand[k, :, depth:] = low

        load_block(step).wait()
        b_high, b_low = split(blocks[slot])
        value = dot(left_hand[k], jnp.concatenate([b_high, b_high], axis=0))
        value += dot(left_hand[k, :, :depth], b_low)

        @pl.when(k == 0)
        def _():
            acc[...] = value

        @pl.when(k > 0)
        def _():
            acc[...] += value

        @pl.when(step + 2 * CHUNKS < steps)
        def _():
            load_block(step + 2 * CHUNKS).start()

        @pl.when((k == 0) & (j >= 1))
        def _():
            gather_swap(j - 1)

            @pl.when(jnp.logical_not(inner))
            def _():
                hop(j - 1).start()

        for when, passed in FORWARD:

            @pl.when((step == when) & inner)
            def _():
                forward(passed)

        @pl.when(k == CHUNKS - 1)
        def _():
            left, right = acc[:, :LANES], acc[:, LANES:]
            first = sub == 0
            mine[j] = jnp.where(first, left, right)
            outbox[j] = jnp.where(first, right, left)
            swap(j).start()

    gather_swap(last)

    @pl.when(col > 0)
    def _():
        arrival(0, col).wait_recv()
        mine[last] += arrived[0, col]

    near[...] = mine[last]

    @pl.when(col < last)
    def _():
        arrival(1, col).wait_recv()
        far[...] = arrived[1, col]

    @pl.when(col == last)
    def _():
        far[...] = jnp.zeros_like(far)

    for j in range(cols_n):
        swap(j).wait_send()
        if j < last:
            hop(j).wait_send()


def local(amps, integrals, occ_pairs, slab_pairs, occ_energy, vir_energy):
    rows, depth = amps.shape
    width = integrals.shape[1]
    cols_n, subs = lax.axis_size("col"), lax.axis_size("sub")
    fits = (
        cols_n == 4 and subs == 2 and width == cols_n * subs * LANES
        and depth % (CHUNKS * LANES) == 0 and rows % LANES == 0
        and vir_energy.shape[0] % LANES == 0
    )
    if not fits:
        return plain(amps, integrals, occ_pairs, slab_pairs, occ_energy, vir_energy)
    piece = depth // CHUNKS
    f32, bf16 = jnp.float32, jnp.bfloat16
    dma = pltpu.SemaphoreType.DMA
    vmem = pl.BlockSpec(memory_space=pltpu.VMEM)
    hbm = pl.BlockSpec(memory_space=pl.ANY)
    near, far, denom = pl.pallas_call(
        functools.partial(ladder, cols_n),
        out_shape=[jax.ShapeDtypeStruct((rows, LANES), f32)] * 3,
        in_specs=[hbm, hbm, vmem, vmem, vmem, vmem],
        out_specs=[vmem, vmem, vmem],
        scratch_shapes=[
            pltpu.VMEM((CHUNKS, rows, piece), f32),
            pltpu.VMEM((CHUNKS, rows, 2 * piece), bf16),
            pltpu.VMEM((2 * CHUNKS, piece, 2 * LANES), f32),
            pltpu.VMEM((rows, 2 * LANES), f32),
            pltpu.VMEM((cols_n, rows, LANES), f32),
            pltpu.VMEM((cols_n, rows, LANES), f32),
            pltpu.VMEM((cols_n, rows, LANES), f32),
            pltpu.VMEM((2, cols_n, rows, LANES), f32),
            dma((CHUNKS,)),
            dma((2 * CHUNKS,)),
            dma((cols_n,)),
            dma((cols_n,)),
            dma((cols_n,)),
            dma((2, cols_n)),
        ],
        compiler_params=pltpu.CompilerParams(
            collective_id=0, has_side_effects=True, vmem_limit_bytes=62 * 1024 * 1024
        ),
        cost_estimate=pl.CostEstimate(
            flops=6 * rows * depth * width,
            bytes_accessed=4 * depth * (rows + width),
            transcendentals=0,
        ),
    )(amps, integrals, occ_pairs.T, slab_pairs.T, occ_energy[None, :], vir_energy[None, :])
    residual = near + far
    return residual, residual / denom


def solution(mesh):
    return jax.shard_map(
        local,
        mesh=mesh,
        in_specs=(
            P(("groups", "row"), ("col", "sub")),
            P(("groups", "col", "sub"), None),
            P("row", None),
            P(),
            P("groups"),
            P("groups"),
        ),
        out_specs=(P(("groups", "row"), ("col", "sub")), P(("groups", "row"), ("col", "sub"))),
        check_vma=False,
    )
```

```python
import functools

import jax
import jax.numpy as jnp
from jax import lax
from jax.experimental import pallas as pl
from jax.experimental.pallas import tpu as pltpu
from jax.sharding import PartitionSpec as P

LANES = 128
CHUNKS = 4
FORWARD = ((9, 0), (13, 1), (14, 2))
MESH = pl.DeviceIdType.MESH


def lookup(table, indices):
    places = jnp.arange(table.shape[0], dtype=jnp.int32)
    return jnp.sum(jnp.where(indices[:, None] == places[None, :], table[None, :], 0.0), axis=1)


def pair_energy(table, pairs):
    return lookup(table, pairs[:, 0]) + lookup(table, pairs[:, 1])


def plain(amps, integrals, occ_pairs, slab_pairs, occ_energy, vir_energy):
    width = integrals.shape[1]
    pieces = lax.axis_size(("col", "sub"))
    partial_value = jnp.dot(
        amps, integrals, precision=lax.Precision.HIGH, preferred_element_type=jnp.float32
    )
    residual = lax.psum_scatter(partial_value, ("col", "sub"), scatter_dimension=1, tiled=True)
    columns = width // pieces
    first_col = lax.axis_index(("col", "sub")) * columns
    slab_here = lax.dynamic_slice_in_dim(slab_pairs, first_col, columns, 0)
    denominator = (
        pair_energy(occ_energy, occ_pairs)[:, None] - pair_energy(vir_energy, slab_here)[None, :]
    )
    increment = residual / denominator
    return (residual, increment)


def column_of(row):
    n = row.shape[1]
    here = lax.broadcasted_iota(jnp.int32, (n, n), 0) == lax.broadcasted_iota(jnp.int32, (n, n), 1)
    return jnp.sum(jnp.where(here, jnp.broadcast_to(row, (n, n)), 0.0), axis=1, keepdims=True)


def table_row(table, indices):
    shape = (table.shape[0], indices.shape[1])
    places = lax.broadcasted_iota(jnp.int32, shape, 0)
    picked = jnp.where(places == jnp.broadcast_to(indices, shape), jnp.broadcast_to(table, shape), 0.0)
    return jnp.sum(picked, axis=0, keepdims=True)


def split(values):
    high = values.astype(jnp.bfloat16)
    return high, (values - high.astype(jnp.float32)).astype(jnp.bfloat16)


def dot(a, b):
    return jnp.dot(a, b, preferred_element_type=jnp.float32)


def ladder(
    cols_n, amps, integrals, occ_t, slab_t, occ_e, vir_e, near, far, denom,
    wide, left_hand, blocks, acc, outbox, inbox, mine, arrived,
    wide_sem, block_sem, swap_send, swap_recv, hop_send, hop_recv,
):
    rows = amps.shape[0]
    depth = wide.shape[2]
    last = cols_n - 1
    col, sub = lax.axis_index("col"), lax.axis_index("sub")

    def order(j):
        return (
            (1 - (j + 2) // 3) * last * (1 - col // 2)
            + (j % 2) * (1 - j // 3) * ((3 * col + 2) % 5)
            + (1 - j % 2) * (j // 2) * (1 + col % 2)
            + (j // 3) * col
        )

    def way(j):
        return (1 - j % 2) * (col // 2) + (j % 2) * (col % 2)

    def load_wide(k):
        return pltpu.make_async_copy(
            amps.at[:, pl.ds(pl.multiple_of(k * depth, depth), depth)], wide.at[k], wide_sem.at[k]
        )

    def load_block(step):
        j, k = step // CHUNKS, step % CHUNKS
        slot = step % (2 * CHUNKS)
        return pltpu.make_async_copy(
            integrals.at[
                pl.ds(pl.multiple_of(k * depth, depth), depth),
                pl.ds(pl.multiple_of(order(j) * 2 * LANES, 2 * LANES), 2 * LANES),
            ],
            blocks.at[slot],
            block_sem.at[slot],
        )

    def swap(j):
        return pltpu.make_async_remote_copy(
            src_ref=outbox.at[j], dst_ref=inbox.at[j],
            send_sem=swap_send.at[j], recv_sem=swap_recv.at[j],
            device_id={"sub": 1 - sub}, device_id_type=MESH,
        )

    def hop(j):
        return pltpu.make_async_remote_copy(
            src_ref=mine.at[j], dst_ref=arrived.at[way(j), order(j)],
            send_sem=hop_send.at[j], recv_sem=hop_recv.at[way(j), order(j)],
            device_id={"col": col + 1 - 2 * way(j)}, device_id_type=MESH,
        )

    def arrival(d, target):
        return pltpu.make_async_remote_copy(
            src_ref=mine.at[0], dst_ref=arrived.at[d, target],
            send_sem=hop_send.at[0], recv_sem=hop_recv.at[d, target],
            device_id={"col": col}, device_id_type=MESH,
        )

    @pl.loop(0, CHUNKS)
    def _(k):
        load_wide(k).start()
        load_block(k).start()

    @pl.loop(CHUNKS, 2 * CHUNKS)
    def _(k):
        load_block(k).start()

    barrier = pltpu.get_barrier_semaphore()
    inner = (col > 0) & (col < last)
    pl.semaphore_signal(barrier, inc=1, device_id={"sub": 1 - sub}, device_id_type=MESH)

    @pl.when(col > 0)
    def _():
        pl.semaphore_signal(barrier, inc=1, device_id={"col": col - 1}, device_id_type=MESH)

    @pl.when(col < last)
    def _():
        pl.semaphore_signal(barrier, inc=1, device_id={"col": col + 1}, device_id_type=MESH)

    occ_table = column_of(occ_e[...])
    vir_table = jnp.concatenate(
        [column_of(vir_e[:, at : at + LANES]) for at in range(0, vir_e.shape[1], LANES)], axis=0
    )
    own = pl.multiple_of((2 * col + sub) * LANES, LANES)
    slab = slab_t[:, pl.ds(own, LANES)]
    vir_row = table_row(vir_table, slab[0:1, :]) + table_row(vir_table, slab[1:2, :])
    for at in range(0, rows, LANES):
        pairs = occ_t[:, at : at + LANES]
        occ_row = table_row(occ_table, pairs[0:1, :]) + table_row(occ_table, pairs[1:2, :])
        denom[at : at + LANES, :] = column_of(occ_row) - vir_row

    @pl.when(inner)
    def _():
        pl.semaphore_wait(barrier, 3)

    @pl.when(jnp.logical_not(inner))
    def _():
        pl.semaphore_wait(barrier, 2)

    def gather_swap(j):
        swap(j).wait_recv()
        mine[j] += inbox[j]

    def forward(j):
        arrival(way(j), order(j)).wait_recv()
        mine[j] += arrived[way(j), order(j)]
        hop(j).start()

    acc[...] = jnp.zeros_like(acc)
    steps = cols_n * CHUNKS

    @pl.loop(0, steps)
    def _(step):
        j, k = step // CHUNKS, step % CHUNKS
        slot = step % (2 * CHUNKS)

        @pl.when(step < CHUNKS)
        def _():
            load_wide(k).wait()
            high, low = split(wide[k])
            left_hand[k, :, :depth] = high
            left_hand[k, :, depth:] = low

        load_block(step).wait()
        b_high, b_low = split(blocks[slot])
        value = dot(left_hand[k], jnp.concatenate([b_high, b_high], axis=0))
        value += dot(left_hand[k, :, :depth], b_low)

        acc[...] = jnp.where(k == 0, value, acc[...] + value)

        @pl.when(step + 2 * CHUNKS < steps)
        def _():
            load_block(step + 2 * CHUNKS).start()

        @pl.when((k == 0) & (j >= 1))
        def _():
            gather_swap(j - 1)

            @pl.when(jnp.logical_not(inner))
            def _():
                hop(j - 1).start()

        for when, passed in FORWARD:

            @pl.when((step == when) & inner)
            def _():
                forward(passed)

        @pl.when(k == CHUNKS - 1)
        def _():
            left, right = acc[:, :LANES], acc[:, LANES:]
            first = sub == 0
            mine[j] = jnp.where(first, left, right)
            outbox[j] = jnp.where(first, right, left)
            swap(j).start()

    gather_swap(last)

    @pl.when(col > 0)
    def _():
        arrival(0, col).wait_recv()
        mine[last] += arrived[0, col]

    near[...] = mine[last]

    @pl.when(col < last)
    def _():
        arrival(1, col).wait_recv()
        far[...] = arrived[1, col]

    @pl.when(col == last)
    def _():
        far[...] = jnp.zeros_like(far)

    for j in range(cols_n):
        swap(j).wait_send()
        if j < last:
            hop(j).wait_send()


def local(amps, integrals, occ_pairs, slab_pairs, occ_energy, vir_energy):
    rows, depth = amps.shape
    width = integrals.shape[1]
    cols_n, subs = lax.axis_size("col"), lax.axis_size("sub")
    fits = (
        cols_n == 4 and subs == 2 and width == cols_n * subs * LANES
        and depth % (CHUNKS * LANES) == 0 and rows % LANES == 0
        and vir_energy.shape[0] % LANES == 0
    )
    if not fits:
        return plain(amps, integrals, occ_pairs, slab_pairs, occ_energy, vir_energy)
    piece = depth // CHUNKS
    f32, bf16 = jnp.float32, jnp.bfloat16
    dma = pltpu.SemaphoreType.DMA
    vmem = pl.BlockSpec(memory_space=pltpu.VMEM)
    hbm = pl.BlockSpec(memory_space=pl.ANY)
    near, far, denom = pl.pallas_call(
        functools.partial(ladder, cols_n),
        out_shape=[jax.ShapeDtypeStruct((rows, LANES), f32)] * 3,
        in_specs=[hbm, hbm, vmem, vmem, vmem, vmem],
        out_specs=[vmem, vmem, vmem],
        scratch_shapes=[
            pltpu.VMEM((CHUNKS, rows, piece), f32),
            pltpu.VMEM((CHUNKS, rows, 2 * piece), bf16),
            pltpu.VMEM((2 * CHUNKS, piece, 2 * LANES), f32),
            pltpu.VMEM((rows, 2 * LANES), f32),
            pltpu.VMEM((cols_n, rows, LANES), f32),
            pltpu.VMEM((cols_n, rows, LANES), f32),
            pltpu.VMEM((cols_n, rows, LANES), f32),
            pltpu.VMEM((2, cols_n, rows, LANES), f32),
            dma((CHUNKS,)),
            dma((2 * CHUNKS,)),
            dma((cols_n,)),
            dma((cols_n,)),
            dma((cols_n,)),
            dma((2, cols_n)),
        ],
        compiler_params=pltpu.CompilerParams(
            collective_id=0, has_side_effects=True, vmem_limit_bytes=62 * 1024 * 1024
        ),
        cost_estimate=pl.CostEstimate(
            flops=6 * rows * depth * width,
            bytes_accessed=4 * depth * (rows + width),
            transcendentals=0,
        ),
    )(amps, integrals, occ_pairs.T, slab_pairs.T, occ_energy[None, :], vir_energy[None, :])
    residual = near + far
    return residual, residual / denom


def solution(mesh):
    return jax.shard_map(
        local,
        mesh=mesh,
        in_specs=(
            P(("groups", "row"), ("col", "sub")),
            P(("groups", "col", "sub"), None),
            P("row", None),
            P(),
            P("groups"),
            P("groups"),
        ),
        out_specs=(P(("groups", "row"), ("col", "sub")), P(("groups", "row"), ("col", "sub"))),
        check_vma=False,
    )
```
